128 devices in a mesh: gx: 8 (over z, core), gy: 8 (over y, x_lo), gz: 2 (over x_hi).
Axes of the slice: x: 4 (x_hi: 2, x_lo: 2; x = x_hi * 2 + x_lo), y: 4, z: 4, core: 2. Of those that a mesh axis runs over, the one named last changes fastest.
Arguments:
- atom_feat: bfloat16 [131072, 128], P(('gx', 'gy', 'gz')), may hold values from -6 to 6
- atom_pos: float32 [3, 131072], P(None, ('gx', 'gy', 'gz')), may hold values from 0 to 4
- pair_list: int32 [16, 131072], P(None, ('gx', 'gy', 'gz')), may hold values from 0 to 4479
- halo_rows: int32 [16384], P(('gx', 'gy', 'gz')), may hold values from 0 to 1023
- w_proj: bfloat16 [128, 128], replicated, may hold values from -0.5 to 0.5
- w_radial: float32 [8, 128], replicated, may hold values from -2 to 2
- w_hidden: bfloat16 [128, 128], replicated, may hold values from -0.5 to 0.5
- w_out: float32 [128], replicated, may hold values from -0.5 to 0.5
- centre_charge: float32 [65536], P(('gx', 'gy', 'gz')), may hold values from -6 to 6
- centre_base: int32 [3, 65536], P(None, ('gx', 'gy', 'gz')), may hold values from 0 to 127, as said below
- centre_frac: float32 [3, 65536], P(None, ('gx', 'gy', 'gz')), may hold values from 0 to 1
- green_x: float32 [129], replicated, may hold values from 0.01 to 0.2
- green_y: float32 [129], replicated, may hold values from 0.01 to 0.2
- green_z: float32 [129], replicated, may hold values from 0.01 to 0.2
Outputs:
- atom_out: float32 [4, 131072], P(None, ('gx', 'gy', 'gz'))
- centre_out: float32 [4, 65536], P(None, ('gx', 'gy', 'gz'))
The draws below stay inside these ranges and needn't reach their ends.
Inputs may be any that keep to these rules, and one draw needn't show every extreme that they name: `centre_base`: row 0 lies below 32, row 1 below 32, row 2 below 128; row 2 reaches 127.
All inputs are finite; a program needn't handle non-finite values.
Results may differ from the reference program's by a relative error of at most 0.02.
Values may be sent and summed in bfloat16 or wider, within the bound.
A program may use at most 128 MiB of HBM per device.

```python
import math
import jax
import jax.numpy as jnp
from jax import lax

C = 128
NB = 8
M = 256
NEIGH = 16
ATOM_DEV = 1024
SEND = 128
WC_DEV = 512
ATOMS = 131072
SENDS = 16384
CENTRES = 65536
TABLE = 4480
HALF = 129
BX = 32
BY = 32
BZ = 128
N_GX = 8
N_GY = 8
N_GZ = 2


def draw_centre_base(key, part):
    key = jax.random.fold_in(key, 11)
    keys = jax.random.split(key, 3)
    first = jax.random.randint(keys[0], (CENTRES,), 0, BX)
    second = jax.random.randint(keys[1], (CENTRES,), 0, BY)
    third = jax.random.randint(keys[2], (CENTRES,), 0, BZ)
    third = third.at[0].set(BZ - 1)
    return jnp.stack([first, second, third]).astype(jnp.int32)


def touch_ends(entries, key, smallest, top_value):
    place = [jax.random.randint(jax.random.fold_in(key, axis), (), 0, length) for axis, length in enumerate(entries.shape)]
    main_axis = entries.shape.index(max(entries.shape))
    beside = place[:main_axis] + [(place[main_axis] + 1) % entries.shape[main_axis]] + place[main_axis + 1:]
    return entries.at[tuple(place)].set(smallest).at[tuple(beside)].set(top_value)


def block_levels(own_key, dims, pieces, smallest, high):
    loudness = 1.0
    for position, blocks in pieces:
        heights = jax.random.uniform(jax.random.fold_in(jax.random.fold_in(own_key, 6), position), (blocks,), jnp.float32, smallest / len(pieces), high / len(pieces))
        loudness = loudness * jnp.repeat(jnp.exp(heights), dims[position] // blocks).reshape((-1,) + (1,) * (len(dims) - 1 - position))
    return loudness


def noise(rng, shape, deviation, most, pieces=(), kind=jnp.bfloat16):
    gain = block_levels(rng, shape, pieces, -0.22, 0.18) if pieces else 1.0
    result = jax.random.normal(rng, shape, jnp.float32) * deviation * gain
    return jnp.minimum(jnp.maximum(result, -most), most).astype(kind)


def setup_inputs(seed: int = 0) -> dict:
    key_list = jax.random.split(jax.random.key(seed), 15)
    return {
        "atom_feat": noise(key_list[0], (ATOMS, C), 1.0, 6.0, ((0, 128),)),
        "atom_pos": jnp.clip(4.0 * jax.random.uniform(key_list[1], (3, ATOMS), jnp.float32) ** block_levels(key_list[1], (3, ATOMS), ((1, 128),), -0.2, 0.2), 0.0, 4.0),
        "pair_list": touch_ends(jax.random.randint(key_list[2], (NEIGH, ATOMS), 0, TABLE), jax.random.fold_in(key_list[2], 1), 0, TABLE - 1).astype(jnp.int32),
        "halo_rows": touch_ends(jax.random.randint(key_list[3], (SENDS,), 0, ATOM_DEV), jax.random.fold_in(key_list[3], 1), 0, ATOM_DEV - 1).astype(jnp.int32),
        "w_proj": noise(key_list[4], (C, C), C ** -0.5, 0.5),
        "w_radial": noise(key_list[5], (NB, C), NB ** -0.5, 2.0, (), jnp.float32),
        "w_hidden": noise(key_list[6], (C, C), C ** -0.5, 0.5),
        "w_out": noise(key_list[7], (C,), C ** -0.5, 0.5, (), jnp.float32),
        "centre_charge": noise(key_list[8], (CENTRES,), 1.0, 6.0, ((0, 128),), jnp.float32),
        "centre_base": draw_centre_base(jax.random.fold_in(key_list[14], 71), 0),
        "centre_frac": jnp.clip(1.0 * jax.random.uniform(key_list[10], (3, CENTRES), jnp.float32) ** block_levels(key_list[10], (3, CENTRES), ((1, 128),), -0.2, 0.2), 0.0, 1.0),
        "green_x": jnp.clip(jnp.exp(jax.random.uniform(key_list[11], (HALF,), jnp.float32, math.log(0.01), math.log(0.2))), 0.01, 0.2),
        "green_y": jnp.clip(jnp.exp(jax.random.uniform(key_list[12], (HALF,), jnp.float32, math.log(0.01), math.log(0.2))), 0.01, 0.2),
        "green_z": jnp.clip(jnp.exp(jax.random.uniform(key_list[13], (HALF,), jnp.float32, math.log(0.01), math.log(0.2))), 0.01, 0.2),
    }


SOFTEN = 0.5
RADIUS = 12.0
ENVELOPE = 6.0
BRICK = 4.0
HIGH = lax.Precision.HIGHEST

def silu_slope(value):
    sig = jax.nn.sigmoid(value)
    return sig * (1.0 + value * (1.0 - sig))

def pair_terms(own_proj, table_proj, own_pos, table_pos, pairs, w_radial, w_hidden, w_out):
    neigh, atoms = pairs.shape
    width = own_proj.shape[1]
    flat = pairs.reshape(-1)
    other = jnp.take(table_proj, flat, axis=0)
    other_pos = jnp.take(table_pos, flat, axis=1).reshape(3, neigh, atoms)
    disp = other_pos - own_pos[:, None, :]
    dist = jnp.sqrt(lax.optimization_barrier(jnp.sum(disp * disp, axis=0)) + SOFTEN * SOFTEN).reshape(-1)
    orders = jnp.arange(1, w_radial.shape[0] + 1, dtype=jnp.float32) * (jnp.pi / RADIUS)
    phase = dist[:, None] * orders[None, :]
    basis = jnp.sin(phase) / dist[:, None]
    basis_slope = (orders[None, :] * jnp.cos(phase) - jnp.sin(phase) / dist[:, None]) / dist[:, None]
    start = (other.reshape(neigh, atoms, width) + own_proj[None]).reshape(-1, width)
    start = start + jnp.dot(basis, w_radial, precision=HIGH)
    hidden = jax.nn.silu(start).astype(jnp.bfloat16)
    inner = jnp.dot(hidden, w_hidden, preferred_element_type=jnp.float32)
    score = jnp.dot(jax.nn.silu(inner), w_out, precision=HIGH)
    envelope = jnp.exp(-(dist / ENVELOPE) ** 2)
    energy = 0.5 * lax.optimization_barrier(jnp.sum((envelope * score).reshape(neigh, atoms), axis=0))
    back = (w_out[None, :] * silu_slope(inner)).astype(jnp.bfloat16)
    grad = jnp.dot(back, w_hidden.T, preferred_element_type=jnp.float32) * silu_slope(start)
    radial_grad = jnp.dot(grad, w_radial.T, precision=HIGH)
    dscore = lax.optimization_barrier(jnp.sum(radial_grad * basis_slope, axis=1))
    dpair = envelope * dscore - 2.0 * dist / (ENVELOPE * ENVELOPE) * envelope * score
    push = (dpair / dist).reshape(neigh, atoms)
    force = lax.optimization_barrier(jnp.sum(push[None] * disp, axis=1))
    return jnp.concatenate([energy[None], force], axis=0)

def spline_weights(frac):
    rest = 1.0 - frac
    return (rest * rest * rest / 6.0, (3.0 * frac ** 3 - 6.0 * frac * frac + 4.0) / 6.0, (-3.0 * frac ** 3 + 3.0 * frac * frac + 3.0 * frac + 1.0) / 6.0, frac ** 3 / 6.0)

def spline_slopes(frac):
    rest = 1.0 - frac
    return (-0.5 * rest * rest, (3.0 * frac * frac - 4.0 * frac) / 2.0, (-3.0 * frac * frac + 2.0 * frac + 1.0) / 2.0, 0.5 * frac * frac)

def folded_values(table):
    waves = jnp.arange(M, dtype=jnp.int32)
    folded = jnp.minimum(waves, M - waves).astype(jnp.int32)
    return jnp.take(table, folded, axis=0)

def reference(atom_feat, atom_pos, pair_list, halo_rows, w_proj, w_radial, w_hidden, w_out, centre_charge, centre_base, centre_frac, green_x, green_y, green_z):
    proj = jnp.dot(atom_feat, w_proj, preferred_element_type=jnp.float32)
    devices = N_GX * N_GY * N_GZ

    def one_device(index):
        row_a = index // (N_GY * N_GZ)
        row_b = index // N_GZ % N_GY
        row_c = index % N_GZ
        own_proj = lax.dynamic_slice_in_dim(proj, index * ATOM_DEV, ATOM_DEV, 0)
        own_pos = lax.dynamic_slice_in_dim(atom_pos, index * ATOM_DEV, ATOM_DEV, 1)
        pairs = lax.dynamic_slice_in_dim(pair_list, index * ATOM_DEV, ATOM_DEV, 1)
        proj_parts = [own_proj]
        pos_parts = [own_pos]
        for step_x in (-1, 0, 1):
            for step_y in (-1, 0, 1):
                for step_z in (-1, 0, 1):
                    peer = ((row_a + step_x) % N_GX * N_GY + (row_b + step_y) % N_GY) * N_GZ + (row_c + step_z) % N_GZ
                    peer = peer.astype(jnp.int32)
                    rows = lax.dynamic_slice_in_dim(halo_rows, peer * SEND, SEND, 0) + peer * ATOM_DEV
                    proj_parts.append(jnp.take(proj, rows, axis=0))
                    offset = jnp.array([step_x, step_y, step_z], jnp.float32) * BRICK
                    pos_parts.append(jnp.take(atom_pos, rows, axis=1) + offset[:, None])
        table_proj = jnp.concatenate(proj_parts, axis=0)
        table_pos = jnp.concatenate(pos_parts, axis=1)
        return pair_terms(own_proj, table_proj, own_pos, table_pos, pairs, w_radial, w_hidden, w_out)
    per_device = lax.map(one_device, jnp.arange(devices, dtype=jnp.int32))
    atom_out = jnp.transpose(per_device, (1, 0, 2)).reshape(4, -1)
    owner = jnp.arange(CENTRES, dtype=jnp.int32) // WC_DEV
    brick = jnp.stack([owner // (N_GY * N_GZ), owner // N_GZ % N_GY, owner % N_GZ])
    extent = jnp.array([BX, BY, BZ], jnp.int32)
    first = brick * extent[:, None] + centre_base - 1
    weights = [spline_weights(centre_frac[k]) for k in range(3)]
    slopes = [spline_slopes(centre_frac[k]) for k in range(3)]
    rho = jnp.zeros((M, M, M), jnp.float32)
    for i in range(4):
        for j in range(4):
            for k in range(4):
                rho = rho.at[(first[0] + i) % M, (first[1] + j) % M, (first[2] + k) % M].add(centre_charge * weights[0][i] * weights[1][j] * weights[2][k])
    stiff = folded_values(green_x)[:, None, None] + folded_values(green_y)[None, :, None] + folded_values(green_z)[None, None, :]
    spectrum = jnp.fft.fftn(rho) * (1.0 / stiff)
    phi = jnp.real(jnp.fft.ifftn(spectrum)).astype(jnp.float32)
    value = jnp.zeros((CENTRES,), jnp.float32)
    grad_x = jnp.zeros((CENTRES,), jnp.float32)
    grad_y = jnp.zeros((CENTRES,), jnp.float32)
    grad_z = jnp.zeros((CENTRES,), jnp.float32)
    for i in range(4):
        for j in range(4):
            for k in range(4):
                here = phi[(first[0] + i) % M, (first[1] + j) % M, (first[2] + k) % M]
                value = value + weights[0][i] * weights[1][j] * weights[2][k] * here
                grad_x = grad_x + slopes[0][i] * weights[1][j] * weights[2][k] * here
                grad_y = grad_y + weights[0][i] * slopes[1][j] * weights[2][k] * here
                grad_z = grad_z + weights[0][i] * weights[1][j] * slopes[2][k] * here
    centre_out = jnp.stack([value, centre_charge * grad_x, centre_charge * grad_y, centre_charge * grad_z])
    return (atom_out, centre_out)
```

```python
import functools

import jax
import jax.numpy as jnp
import numpy as np
from jax import lax
from jax.experimental import pallas as pl
from jax.experimental.pallas import tpu as pltpu
from jax.sharding import PartitionSpec as P

M = 256
ATOMS = 1024
SEND = 128
WC = 512
NEIGH = 16
BLOCK = 144
MESH = pl.DeviceIdType.MESH
VMEM = pltpu.VMEM
F32 = jnp.float32
BF16 = jnp.bfloat16
ROWS = 12
SIDE = 24
NN = (((1,), (0,)), ((), ()))
NT = (((1,), (1,)), ((), ()))


def real_basis(index, points):
    wave = np.where(index <= 128, index, index - 128)
    scale = np.where((index == 0) | (index == 128), 1.0 / 16.0, np.sqrt(2.0) / 16.0)
    angle = 2.0 * np.pi * ((wave[:, None] * points[None, :]) % M) / M
    return scale[:, None] * np.where((index <= 128)[:, None], np.cos(angle), np.sin(angle))


def halves(value):
    value = np.asarray(value, np.float32)
    high = value.astype(jnp.bfloat16)
    low = (value - high.astype(np.float32)).astype(jnp.bfloat16)
    return np.stack([high, low])


def constants():
    waves = np.arange(M)
    base_z = np.zeros((2, 128, 144))
    for parity in range(2):
        owner = 2 * np.arange(64) + parity
        index = np.concatenate([owner, owner + 128])
        base_z[parity] = real_basis(index, np.arange(144) - 1)
    along = np.zeros((8, 128, 768))
    for brick in range(8):
        points = (32 * brick + np.arange(35) - 1) % M
        table = real_basis(waves, points)
        for part in range(3):
            along[brick, 40 * part : 40 * part + 35, 256 * part : 256 * part + 256] = table.T
    across = np.zeros((2, 256, 3, 8, 2, ROWS))
    for brick in range(8):
        for part in range(3):
            for row in range(ROWS):
                shift = 3 * row + part
                if shift < 35:
                    value = real_basis(waves, np.array([(32 * brick + shift - 1) % M]))[:, 0]
                    across[0, :, part, brick, 0, row] = value
                    across[1, :, part, brick, 1, row] = value
    across = across.reshape(512, 576)
    return halves(base_z), halves(along.reshape(1024, 768)), halves(across), halves(across.T)


def split(value):
    high = value.astype(BF16)
    return high, (value - high.astype(F32)).astype(BF16)


def dot(a, b, dims):
    return lax.dot_general(a, b, dims, preferred_element_type=F32)


def dot3(a, b, dims):
    return dot(a[0], b[0], dims) + (dot(a[1], b[0], dims) + dot(a[0], b[1], dims))


def position():
    return lax.axis_index("gx"), lax.axis_index("gy"), lax.axis_index("gz")


def spline_weights(frac):
    rest = 1.0 - frac
    square = frac * frac
    cube = square * frac
    return (
        rest * rest * rest / 6.0,
        (3.0 * cube - 6.0 * square + 4.0) / 6.0,
        (-3.0 * cube + 3.0 * square + 3.0 * frac + 1.0) / 6.0,
        cube / 6.0,
    )


def spline_slopes(frac):
    rest = 1.0 - frac
    square = frac * frac
    return (
        -0.5 * rest * rest,
        (3.0 * square - 4.0 * frac) / 2.0,
        (-3.0 * square + 2.0 * frac + 1.0) / 2.0,
        0.5 * square,
    )


def spline_table(base, weights, length):
    points = lax.broadcasted_iota(jnp.int32, (length, base.shape[1]), 0).astype(F32)
    away = points - base
    table = jnp.where(away == 0.0, weights[0], 0.0)
    for shift in range(1, 4):
        table = jnp.where(away == float(shift), weights[shift], table)
    return table


def around(a, b, c, step):
    return (a + step[0] + 8) % 8, (b + step[1] + 8) % 8, (c + step[2]) % 2


def block_of(step):
    return (step[0] + 1) * 6 + (step[1] + 1) * 2 + abs(step[2])


STEPS = [
    (dx, dy, dz)
    for dx in (-1, 0, 1)
    for dy in (-1, 0, 1)
    for dz in (0, 1)
    if (dx, dy, dz) != (0, 0, 0)
]


def halo_kernel(rows_ref, feat_ref, pos_ref, centre_ref, near_ref, other_ref,
                wide, mine, send_sem, recv_sem, csend, crecv):
    a, b, c = position()
    barrier = pltpu.get_barrier_semaphore()
    for step in STEPS:
        pl.semaphore_signal(barrier, inc=1, device_id=around(a, b, c, step), device_id_type=MESH)
    wide[...] = feat_ref[...].astype(F32)

    def pick(group, _):
        base = group * 8
        for s in range(8):
            row = rows_ref[base + s]
            mine[pl.ds(base + s, 1), :] = wide[pl.ds(row, 1), :]
        return 0

    lax.fori_loop(0, SEND // 8, pick, 0)
    rows = jnp.zeros((8, SEND), jnp.int32)
    lane = lax.broadcasted_iota(jnp.int32, (8, SEND), 1)
    for s in range(SEND):
        rows = jnp.where(lane == s, rows_ref[s], rows)
    chosen = jnp.zeros((8, SEND), F32)
    place, inside = rows // 128, rows % 128
    for chunk in range(ATOMS // 128):
        part = jnp.concatenate(
            [pos_ref[:, chunk * 128 : chunk * 128 + 128], jnp.zeros((5, 128), F32)], axis=0
        )
        found = jnp.take_along_axis(part, inside, axis=1)
        chosen = jnp.where(place == chunk, found, chosen)
    first = chosen.astype(BF16).astype(F32)
    second = (chosen - first).astype(BF16).astype(F32)
    third = (chosen - first) - second
    own = block_of((0, 0, 0))
    near_ref[own, 0:128, :] = mine[...].astype(BF16)
    near_ref[own, 128:144, :] = jnp.concatenate(
        [first[0:3], second[0:3], third[0:3], jnp.zeros((7, 128), F32)], axis=0
    ).astype(BF16)
    pl.semaphore_wait(barrier, len(STEPS))
    centre = pltpu.make_async_remote_copy(
        centre_ref, other_ref, csend, crecv, device_id=(a, b, (c + 1) % 2), device_id_type=MESH
    )
    centre.start()
    for step in STEPS:
        back = block_of((-step[0], -step[1], step[2]))
        pltpu.make_async_remote_copy(
            near_ref.at[own], near_ref.at[back], send_sem, recv_sem,
            device_id=around(a, b, c, step), device_id_type=MESH,
        ).start()
    centre.wait()
    pltpu.make_async_remote_copy(
        near_ref.at[pl.ds(0, 17)], near_ref.at[pl.ds(0, 17)], send_sem, recv_sem,
        device_id=(a, b, (c + 1) % 2), device_id_type=MESH,
    ).wait()


def exchange_kernel(x_ref, o_ref, send_sem, recv_sem):
    a, b, c = position()
    me = a * 8 + b
    barrier = pltpu.get_barrier_semaphore()

    def greet(step, _):
        to = (me + step) % 64
        pl.semaphore_signal(barrier, inc=1, device_id=(to // 8, to % 8, c), device_id_type=MESH)
        return 0

    lax.fori_loop(1, 64, greet, 0)
    pl.semaphore_wait(barrier, 63)

    def send(step, _):
        to = (me + step) % 64
        pltpu.make_async_remote_copy(
            x_ref.at[to], o_ref.at[me], send_sem, recv_sem,
            device_id=(to // 8, to % 8, c), device_id_type=MESH,
        ).start()
        return 0

    lax.fori_loop(1, 64, send, 0)
    o_ref[pl.ds(me, 1)] = x_ref[pl.ds(me, 1)]
    to = (me + 1) % 64
    pltpu.make_async_remote_copy(
        x_ref.at[pl.ds(0, 63)], o_ref.at[pl.ds(0, 63)], send_sem, recv_sem,
        device_id=(to // 8, to % 8, c), device_id_type=MESH,
    ).wait()


def spread_kernel(own_ref, other_ref, basez_ref, send_ref, whigh_ref, wlow_ref, table_ref):
    _, _, c = position()
    sign = jnp.where(c == 1, -1.0, 1.0)
    centre = jnp.concatenate([own_ref[...], other_ref[...]], axis=1)
    own = lax.broadcasted_iota(jnp.int32, (1, 2 * WC), 1) < WC
    charge = centre[0:1] * jnp.where(own, sign, 1.0)
    for d in range(2):
        base, frac = centre[1 + d : 2 + d], centre[4 + d : 5 + d]
        table_ref[40 * d : 40 * d + 40, :] = spline_table(base, spline_weights(frac), 40)
        table_ref[80 + 40 * d : 120 + 40 * d, :] = spline_table(base, spline_slopes(frac), 40)
    base, frac = centre[3:4], centre[6:7]
    bz = (basez_ref[0, c], basez_ref[1, c])
    for part, weights in enumerate((spline_weights(frac), spline_slopes(frac))):
        table = split(spline_table(base, weights, 144))
        high, low = split(dot3(bz, table, NN))
        whigh_ref[:, 1024 * part : 1024 * part + 1024] = high
        wlow_ref[:, 1024 * part : 1024 * part + 1024] = low
    wave = (whigh_ref[:, 0:1024], wlow_ref[:, 0:1024])
    along_y = table_ref[40:80, :] * charge
    gap = jnp.zeros((8, 2 * WC), F32)
    for row in range(0, ROWS, 2):
        pieces = []
        for part in range(6):
            shift = 3 * row + part
            pieces.append(along_y * table_ref[shift : shift + 1, :])
            if part % 3 == 2:
                pieces.append(gap)
        plane = split(jnp.concatenate(pieces, axis=0))
        waves = dot3(wave, plane, NT)
        for q in range(2):
            for h in range(2):
                send_ref[pl.ds(q * ROWS + row + h, 64, stride=SIDE), :] = waves[
                    64 * q : 64 * q + 64, 128 * h : 128 * h + 128
                ]


def filter_kernel(recv_ref, green_ref, along_ref, across_ref, across_t_ref, send_ref):
    a, b, c = position()
    owner = (a * 8 + b) * 2 + c
    total = jnp.zeros((192, 768), F32)
    for pair in range(4):
        parts = [recv_ref[:, 2 * pair + h].reshape(192, 128) for h in range(2)]
        left = split(jnp.concatenate(parts, axis=1))
        right = tuple(along_ref[h, 256 * pair : 256 * pair + 256, :] for h in range(2))
        total = total + dot3(left, right, NN)
    stacked = split(jnp.concatenate([total[:, 256 * i : 256 * i + 256] for i in range(3)], axis=0))
    spectrum = dot3((across_ref[0], across_ref[1]), stacked, NN)
    row = lax.broadcasted_iota(jnp.int32, (M, M), 0)
    col = lax.broadcasted_iota(jnp.int32, (M, M), 1)
    down = jnp.sum(jnp.where(row == col, green_ref[0:1, :], 0.0), axis=1, keepdims=True)
    lanes = lax.broadcasted_iota(jnp.int32, (1, M), 1)
    second = jnp.where(owner == 0, 128, owner)
    planes = []
    for q, wave in enumerate((owner, second)):
        level = jnp.sum(jnp.where(lanes == wave, green_ref[2:3, :], 0.0), axis=1, keepdims=True)
        stiff = (down + green_ref[1:2, :]) + level
        planes.append(spectrum[256 * q : 256 * q + 256] / stiff)
    filtered = split(jnp.concatenate(planes, axis=0))
    space = dot3((across_t_ref[0], across_t_ref[1]), filtered, NN)
    space = split(jnp.concatenate([space[192 * i : 192 * i + 192] for i in range(3)], axis=1))
    for pair in range(4):
        right = tuple(along_ref[h, 256 * pair : 256 * pair + 256, :] for h in range(2))
        out = dot3(space, right, NT)
        for h in range(2):
            send_ref[:, 2 * pair + h] = out[:, 128 * h : 128 * h + 128].reshape(8, SIDE, 128)


def gather_centres(recv_ref, whigh_ref, wlow_ref, table_ref):
    sums = [jnp.zeros((8, 2 * WC), F32) for _ in range(4)]
    wave = (whigh_ref[...], wlow_ref[...])
    for row in range(ROWS):
        field = jnp.concatenate(
            [recv_ref[pl.ds(q * ROWS + row, 64, stride=SIDE), :] for q in range(2)], axis=0
        )
        local = dot3(split(field.T), wave, NN)
        for part in range(3):
            shift = 3 * row + part
            if shift >= 35:
                continue
            flat, steep, upright = 0.0, 0.0, 0.0
            for h in range(5):
                at = 40 * part + 8 * h
                value, slope = local[at : at + 8, 0:1024], local[at : at + 8, 1024:2048]
                weight = table_ref[40 + 8 * h : 48 + 8 * h, :]
                flat = flat + value * weight
                steep = steep + value * table_ref[120 + 8 * h : 128 + 8 * h, :]
                upright = upright + slope * weight
            weight = table_ref[shift : shift + 1, :]
            sums[0] = sums[0] + flat * weight
            sums[1] = sums[1] + flat * table_ref[80 + shift : 81 + shift, :]
            sums[2] = sums[2] + steep * weight
            sums[3] = sums[3] + upright * weight
    return jnp.concatenate([jnp.sum(s, axis=0, keepdims=True) for s in sums], axis=0)


def centre_kernel(recv_ref, whigh_ref, wlow_ref, table_ref, own_ref, out_ref, half, got, send_sem, recv_sem):
    a, b, c = position()
    barrier = pltpu.get_barrier_semaphore()
    partner = (a, b, (c + 1) % 2)
    pl.semaphore_signal(barrier, inc=1, device_id=partner, device_id_type=MESH)
    sums = gather_centres(recv_ref, whigh_ref, wlow_ref, table_ref)
    half[0:4, :] = sums[:, WC:]
    half[4:8, :] = jnp.zeros((4, WC), F32)
    pl.semaphore_wait(barrier, 1)
    copy = pltpu.make_async_remote_copy(half, got, send_sem, recv_sem, device_id=partner, device_id_type=MESH)
    copy.start()
    mine = sums[:, :WC] * jnp.where(c == 1, -1.0, 1.0)
    copy.wait()
    whole = mine + got[0:4, :]
    charge = own_ref[0:1, :]
    out_ref[...] = jnp.concatenate([whole[0:1], whole[1:4] * charge], axis=0)


CHUNK = 256


def pair_setup(feat_ref, near_ref, pos_ref, wproj_ref, pairs_ref, table, own_t, place, disp, dist, basis, slope):
    weight = wproj_ref[...]
    for chunk in range(8):
        rows = 0.5 * dot(feat_ref[128 * chunk : 128 * chunk + 128, :], weight, NN)
        table[128 * chunk : 128 * chunk + 128, :] = rows
        own_t[:, 128 * chunk : 128 * chunk + 128] = rows.T
        for d in range(3):
            place[40 * d + chunk : 40 * d + chunk + 1, :] = pos_ref[d : d + 1, 128 * chunk : 128 * chunk + 128]
    for dx in range(3):
        for dy in range(3):
            for dz in range(2):
                block = dx * 6 + dy * 2 + dz
                rows = 0.5 * dot(near_ref[block, 0:128, :], weight, NN)
                parts = near_ref[block, 128:144, :].astype(F32)
                where = (parts[0:3] + parts[3:6]) + parts[6:9]
                for sz in ((0,), (-1, 1))[dz]:
                    e = dx * 9 + dy * 3 + sz + 1
                    table[1024 + 128 * e : 1152 + 128 * e, :] = rows
                    for d, shift in enumerate((dx - 1, dy - 1, sz)):
                        place[40 * d + 8 + e : 40 * d + 9 + e, :] = where[d : d + 1] + 4.0 * shift

    def locate(tile, _):
        lanes = pl.ds(pl.multiple_of(tile * 128, 128), 128)
        for half in range(2):
            index = pairs_ref[8 * half : 8 * half + 8, lanes]
            chunk, inside = index // 128, index % 128
            found = [jnp.zeros((8, 128), F32)] * 3
            for k in range(35):
                here = chunk == k
                for d in range(3):
                    row = jnp.broadcast_to(place[40 * d + k : 40 * d + k + 1, :], (8, 128))
                    found[d] = jnp.where(here, jnp.take_along_axis(row, inside, axis=1), found[d])
            square = 0.0
            for d in range(3):
                away = found[d] - pos_ref[d : d + 1, lanes]
                disp[16 * d + 8 * half : 16 * d + 8 * half + 8, lanes] = away
                square = square + away * away
            length = jnp.sqrt(square + 0.25)
            dist[8 * half : 8 * half + 8, lanes] = length
            inverse = 1.0 / length
            theta = length * (np.pi / 12.0)
            sine, cosine = jnp.sin(theta), jnp.cos(theta)
            twice = 2.0 * cosine
            s0, s1, c0, c1 = 0.0, sine, 1.0, cosine
            for m in range(1, 9):
                base = s1 * inverse
                at = pl.ds(128 * tile + 64 * half + m - 1, 8, stride=8)
                basis[at, :] = base
                slope[at, :] = (float(m * np.pi / 12.0) * c1 - base) * inverse
                s0, s1 = s1, twice * s1 - s0
                c0, c1 = c1, twice * c1 - c0
        return 0

    lax.fori_loop(0, 8, locate, 0)


def pair_chunks(first, last, index_ref, table, own_t, basis, slope, wrad_ref, wh_ref, wht_ref, wout_ref,
                rows, score, dscore):
    per = ATOMS // CHUNK
    wout = wout_ref[...]

    def one(step, _):
        slot = step // per
        start = pl.multiple_of((step % per) * CHUNK, CHUNK)
        lanes = pl.ds(start, CHUNK)
        for r in range(CHUNK):
            rows[r : r + 1, :] = table[pl.ds(index_ref[slot, start + r], 1), :]

        def stack(table):
            tile = (step % per) * (CHUNK // 128)
            value = jnp.concatenate(
                [table[pl.ds(pl.multiple_of(128 * (tile + t) + 8 * slot, 8), 8), :] for t in range(CHUNK // 128)],
                axis=1,
            )
            high = value.astype(BF16).astype(F32)
            return jnp.concatenate([high, value - high, high], axis=0).astype(BF16)

        radial = dot(wrad_ref[...], stack(basis), NN)
        grad_radial = dot(wrad_ref[...], stack(slope), NN)
        half = (rows[...].T + own_t[:, lanes]) + radial
        tan = jnp.tanh(half)
        up = 1.0 + tan
        hidden = (half * up).astype(BF16)
        inner = dot(wht_ref[...], hidden, NN)
        tan2 = jnp.tanh(inner)
        weighted = wout * (1.0 + tan2)
        score[pl.ds(slot, 1), lanes] = jnp.sum(weighted * inner, axis=0, keepdims=True)
        back = (weighted * (1.0 + inner * (1.0 - tan2))).astype(BF16)
        grad = dot(wh_ref[...], back, NN)
        bend = up * (1.0 + half * (1.0 - tan))
        dscore[pl.ds(slot, 1), lanes] = jnp.sum(grad * bend * grad_radial, axis=0, keepdims=True)
        return 0

    lax.fori_loop(first, last, one, 0)


def pair_finish(disp, dist, score, dscore, out_ref):
    length = dist[...]
    env = jnp.exp(-((length / 6.0) * (length / 6.0)))
    energy = env * score[...]
    push = (env * dscore[...] - 2.0 * length / 36.0 * energy) / length
    out_ref[0:1, :] = 0.5 * jnp.sum(energy, axis=0, keepdims=True)
    for d in range(3):
        out_ref[1 + d : 2 + d, :] = jnp.sum(push * disp[16 * d : 16 * d + 16, :], axis=0, keepdims=True)


def pair_kernel(index_ref, pairs_ref, feat_ref, near_ref, pos_ref, wproj_ref, wrad_ref, wh_ref, wht_ref, wout_ref,
                out_ref, table, own_t, place, disp, dist, basis, slope, rows, score, dscore):
    pair_setup(feat_ref, near_ref, pos_ref, wproj_ref, pairs_ref, table, own_t, place, disp, dist, basis, slope)
    pair_chunks(0, NEIGH * ATOMS // CHUNK, index_ref, table, own_t, basis, slope, wrad_ref, wh_ref, wht_ref,
                wout_ref, rows, score, dscore)
    pair_finish(disp, dist, score, dscore, out_ref)


PAIR_SCRATCH = [
    VMEM((4480, 128), F32), VMEM((128, ATOMS), F32), VMEM((120, 128), F32), VMEM((48, ATOMS), F32),
    VMEM((16, ATOMS), F32), VMEM((1024, 128), F32), VMEM((1024, 128), F32), VMEM((CHUNK, 128), F32),
    VMEM((16, ATOMS), F32), VMEM((16, ATOMS), F32),
]


def call(kernel, outs, args, scratch=(), collective=None, smem=()):
    params = dict(vmem_limit_bytes=56 << 20)
    if collective is not None:
        params.update(collective_id=collective, has_side_effects=True)
    spec = pl.BlockSpec(memory_space=VMEM)
    many = isinstance(outs, (list, tuple))
    return pl.pallas_call(
        kernel,
        out_shape=outs,
        in_specs=[pl.BlockSpec(memory_space=pltpu.SMEM) if i in smem else spec for i in range(len(args))],
        out_specs=[spec] * len(outs) if many else spec,
        scratch_shapes=list(scratch),
        compiler_params=pltpu.CompilerParams(**params),
    )(*args)


def shape(*dims, dtype=F32):
    return jax.ShapeDtypeStruct(dims, dtype)


DMA = pltpu.SemaphoreType.DMA


def exchange(value):
    return call(exchange_kernel, shape(64, SIDE, 128), (value,), (DMA, DMA), collective=2)


def on_device(base_z, along, across, across_t,
    atom_feat, atom_pos, pair_list, halo_rows, w_proj, w_radial, w_hidden, w_out,
    centre_charge, centre_base, centre_frac, green_x, green_y, green_z,
):
    centre = jnp.concatenate(
        [centre_charge[None], centre_base.astype(F32), centre_frac, jnp.zeros((1, WC), F32)], axis=0
    )
    near, other = call(
        halo_kernel,
        [shape(18, BLOCK, 128, dtype=BF16), shape(8, WC)],
        (halo_rows, atom_feat, atom_pos, centre),
        (VMEM((ATOMS, 128), F32), VMEM((SEND, 128), F32), DMA, DMA, DMA, DMA),
        collective=1, smem=(0,),
    )
    send, whigh, wlow, table = call(
        spread_kernel,
        [shape(64 * SIDE, 128), shape(128, 2048, dtype=BF16), shape(128, 2048, dtype=BF16), shape(160, 1024)],
        (centre, other, base_z),
    )
    got = exchange(send.reshape(64, SIDE, 128))
    fold = lambda g: jnp.concatenate([g, g[1:128]])
    greens = jnp.stack([fold(green_x), fold(green_y), fold(green_z)])
    send = call(
        filter_kernel, shape(8, 8, SIDE, 128), (got.reshape(8, 8, SIDE, 128), greens, along, across, across_t)
    )
    got = exchange(send.reshape(64, SIDE, 128))
    centre_out = call(
        centre_kernel, shape(4, WC), (got.reshape(64 * SIDE, 128), whigh, wlow, table, centre),
        (VMEM((8, WC), F32), VMEM((8, WC), F32), DMA, DMA), collective=3,
    )
    radial = (0.5 * w_radial).T
    radial_high = lax.reduce_precision(radial, 8, 7)
    wrad = jnp.concatenate([radial_high, radial_high, radial - radial_high], axis=1).astype(BF16)
    atom_out = call(
        pair_kernel, shape(4, ATOMS),
        (pair_list, pair_list, atom_feat, near, atom_pos, w_proj, wrad,
         0.5 * w_hidden, (0.5 * w_hidden).T, jnp.broadcast_to(w_out[:, None], (128, CHUNK))),
        PAIR_SCRATCH, smem=(0,),
    )
    return (atom_out, centre_out)


def solution(mesh):
    device = P(("gx", "gy", "gz"))
    late = P(None, ("gx", "gy", "gz"))
    tables = [jnp.asarray(t) for t in constants()]

    def run(*args):
        return jax.shard_map(
            on_device,
            mesh=mesh,
            in_specs=(P(), P(), P(), P(),
                P(("gx", "gy", "gz"), None), late, late, device,
                P(), P(), P(), P(), device, late, late, P(), P(), P(),
            ),
            out_specs=(late, late),
            check_vma=False,
        )(*tables, *args)

    return run
```

```python
import functools

import jax
import jax.numpy as jnp
import numpy as np
from jax import lax
from jax.experimental import pallas as pl
from jax.experimental.pallas import tpu as pltpu
from jax.sharding import PartitionSpec as P

M = 256
ATOMS = 1024
SEND = 128
WC = 512
NEIGH = 16
BLOCK = 144
MESH = pl.DeviceIdType.MESH
VMEM = pltpu.VMEM
F32 = jnp.float32
BF16 = jnp.bfloat16
ROWS = 12
SIDE = 24
NN = (((1,), (0,)), ((), ()))
NT = (((1,), (1,)), ((), ()))


def real_basis(index, points):
    wave = np.where(index <= 128, index, index - 128)
    scale = np.where((index == 0) | (index == 128), 1.0 / 16.0, np.sqrt(2.0) / 16.0)
    angle = 2.0 * np.pi * ((wave[:, None] * points[None, :]) % M) / M
    return scale[:, None] * np.where((index <= 128)[:, None], np.cos(angle), np.sin(angle))


def halves(value):
    value = np.asarray(value, np.float32)
    high = value.astype(jnp.bfloat16)
    low = (value - high.astype(np.float32)).astype(jnp.bfloat16)
    return np.stack([high, low])


def constants():
    waves = np.arange(M)
    base_z = np.zeros((2, 128, 144))
    for parity in range(2):
        owner = 2 * np.arange(64) + parity
        index = np.concatenate([owner, owner + 128])
        base_z[parity] = real_basis(index, np.arange(144) - 1)
    along = np.zeros((8, 128, 768))
    for brick in range(8):
        points = (32 * brick + np.arange(35) - 1) % M
        table = real_basis(waves, points)
        for part in range(3):
            along[brick, 40 * part : 40 * part + 35, 256 * part : 256 * part + 256] = table.T
    across = np.zeros((2, 256, 3, 8, 2, ROWS))
    for brick in range(8):
        for part in range(3):
            for row in range(ROWS):
                shift = 3 * row + part
                if shift < 35:
                    value = real_basis(waves, np.array([(32 * brick + shift - 1) % M]))[:, 0]
                    across[0, :, part, brick, 0, row] = value
                    across[1, :, part, brick, 1, row] = value
    across = across.reshape(512, 576)
    return halves(base_z), halves(along.reshape(1024, 768)), halves(across), halves(across.T)


def split(value):
    high = value.astype(BF16)
    return high, (value - high.astype(F32)).astype(BF16)


def dot(a, b, dims):
    return lax.dot_general(a, b, dims, preferred_element_type=F32)


def dot3(a, b, dims):
    return dot(a[0], b[0], dims) + (dot(a[1], b[0], dims) + dot(a[0], b[1], dims))


def position():
    return lax.axis_index("gx"), lax.axis_index("gy"), lax.axis_index("gz")


def spline_weights(frac):
    rest = 1.0 - frac
    square = frac * frac
    cube = square * frac
    return (
        rest * rest * rest / 6.0,
        (3.0 * cube - 6.0 * square + 4.0) / 6.0,
        (-3.0 * cube + 3.0 * square + 3.0 * frac + 1.0) / 6.0,
        cube / 6.0,
    )


def spline_slopes(frac):
    rest = 1.0 - frac
    square = frac * frac
    return (
        -0.5 * rest * rest,
        (3.0 * square - 4.0 * frac) / 2.0,
        (-3.0 * square + 2.0 * frac + 1.0) / 2.0,
        0.5 * square,
    )


def spline_table(base, weights, length):
    points = lax.broadcasted_iota(jnp.int32, (length, base.shape[1]), 0).astype(F32)
    away = points - base
    table = jnp.where(away == 0.0, weights[0], 0.0)
    for shift in range(1, 4):
        table = jnp.where(away == float(shift), weights[shift], table)
    return table


def around(a, b, c, step):
    return (a + step[0] + 8) % 8, (b + step[1] + 8) % 8, (c + step[2]) % 2


def block_of(step):
    return (step[0] + 1) * 6 + (step[1] + 1) * 2 + abs(step[2])


STEPS = [
    (dx, dy, dz)
    for dx in (-1, 0, 1)
    for dy in (-1, 0, 1)
    for dz in (0, 1)
    if (dx, dy, dz) != (0, 0, 0)
]


CHUNK = 512


def pair_setup(feat_ref, near_ref, pos_ref, wproj_ref, pairs_ref, table, own_t, place, disp, dist, basis, slope):
    weight = wproj_ref[...]
    for chunk in range(8):
        rows = 0.5 * dot(feat_ref[128 * chunk : 128 * chunk + 128, :], weight, NN)
        table[128 * chunk : 128 * chunk + 128, :] = rows
        own_t[:, 128 * chunk : 128 * chunk + 128] = rows.T
        for d in range(3):
            place[40 * d + chunk : 40 * d + chunk + 1, :] = pos_ref[d : d + 1, 128 * chunk : 128 * chunk + 128]
    for dx in range(3):
        for dy in range(3):
            for dz in range(2):
                block = dx * 6 + dy * 2 + dz
                rows = 0.5 * dot(near_ref[block, 0:128, :], weight, NN)
                parts = near_ref[block, 128:144, :].astype(F32)
                where = (parts[0:3] + parts[3:6]) + parts[6:9]
                for sz in ((0,), (-1, 1))[dz]:
                    e = dx * 9 + dy * 3 + sz + 1
                    table[1024 + 128 * e : 1152 + 128 * e, :] = rows
                    for d, shift in enumerate((dx - 1, dy - 1, sz)):
                        place[40 * d + 8 + e : 40 * d + 9 + e, :] = where[d : d + 1] + 4.0 * shift

    def locate(tile, _):
        lanes = pl.ds(pl.multiple_of(tile * 128, 128), 128)
        for half in range(2):
            index = pairs_ref[8 * half : 8 * half + 8, lanes]
            chunk, inside = index // 128, index % 128
            found = [jnp.zeros((8, 128), F32)] * 3
            for k in range(35):
                here = chunk == k
                for d in range(3):
                    row = jnp.broadcast_to(place[40 * d + k : 40 * d + k + 1, :], (8, 128))
                    found[d] = jnp.where(here, jnp.take_along_axis(row, inside, axis=1), found[d])
            square = 0.0
            for d in range(3):
                away = found[d] - pos_ref[d : d + 1, lanes]
                disp[16 * d + 8 * half : 16 * d + 8 * half + 8, lanes] = away
                square = square + away * away
            length = jnp.sqrt(square + 0.25)
            dist[8 * half : 8 * half + 8, lanes] = length
            inverse = 1.0 / length
            theta = length * (np.pi / 12.0)
            sine, cosine = jnp.sin(theta), jnp.cos(theta)
            twice = 2.0 * cosine
            s0, s1, c0, c1 = 0.0, sine, 1.0, cosine
            for m in range(1, 9):
                base = s1 * inverse
                at = pl.ds(128 * tile + 64 * half + m - 1, 8, stride=8)
                basis[at, :] = base
                slope[at, :] = (float(m * np.pi / 12.0) * c1 - base) * inverse
                s0, s1 = s1, twice * s1 - s0
                c0, c1 = c1, twice * c1 - c0
        return 0

    lax.fori_loop(0, 8, locate, 0)


def pair_chunks(first, last, index_ref, table, own_t, basis, slope, wrad_ref, wh_ref, wht_ref, wout_ref,
                rows, score, dscore):
    per = ATOMS // CHUNK
    wout = jnp.concatenate([wout_ref[...]] * (CHUNK // 128), axis=1)

    def fetch(step, into):
        base = step * CHUNK
        for r in range(CHUNK):
            into[r : r + 1, :] = table[pl.ds(index_ref[base + r], 1), :]

    def work(step, rows):
        slot = step // per
        start = pl.multiple_of((step % per) * CHUNK, CHUNK)
        lanes = pl.ds(start, CHUNK)

        def stack(table):
            tile = (step % per) * (CHUNK // 128)
            value = jnp.concatenate(
                [table[pl.ds(pl.multiple_of(128 * (tile + t) + 8 * slot, 8), 8), :] for t in range(CHUNK // 128)],
                axis=1,
            )
            high = value.astype(BF16).astype(F32)
            return jnp.concatenate([high, value - high, high], axis=0).astype(BF16)

        radial = dot(wrad_ref[:, 0:24], stack(basis), NN)
        grad_radial = dot(wrad_ref[:, 0:24], stack(slope), NN)
        half = (rows[...].T + own_t[:, lanes]) + radial
        tan = jnp.tanh(half)
        up = 1.0 + tan
        hidden = (half * up).astype(BF16)
        inner = dot(wht_ref[...], hidden, NN)
        tan2 = jnp.tanh(inner)
        weighted = wout * (1.0 + tan2)
        score[pl.ds(slot, 1), lanes] = jnp.sum(weighted * inner, axis=0, keepdims=True)
        back = (weighted * (1.0 + inner * (1.0 - tan2))).astype(BF16)
        grad = dot(wh_ref[...], back, NN)
        bend = up * (1.0 + half * (1.0 - tan))
        dscore[pl.ds(slot, 1), lanes] = jnp.sum(grad * bend * grad_radial, axis=0, keepdims=True)

    fetch(first, rows[0])

    def one(turn, _):
        step = first + 2 * turn
        fetch(step + 1, rows[1])
        work(step, rows[0])
        fetch(jnp.minimum(step + 2, last - 1), rows[0])
        work(step + 1, rows[1])
        return 0

    lax.fori_loop(0, (last - first) // 2, one, 0)


def pair_finish(disp, dist, score, dscore, out_ref):
    length = dist[...]
    env = jnp.exp(-((length / 6.0) * (length / 6.0)))
    energy = env * score[...]
    push = (env * dscore[...] - 2.0 * length / 36.0 * energy) / length
    out_ref[0:1, :] = 0.5 * jnp.sum(energy, axis=0, keepdims=True)
    for d in range(3):
        out_ref[1 + d : 2 + d, :] = jnp.sum(push * disp[16 * d : 16 * d + 16, :], axis=0, keepdims=True)


def offer(rows_ref, feat_ref, pos_ref, wide, mine, block):
    wide[...] = feat_ref[...].astype(F32)

    def pick(group, _):
        base = group * 8
        for s in range(8):
            mine[pl.ds(base + s, 1), :] = wide[pl.ds(rows_ref[base + s], 1), :]
        return 0

    lax.fori_loop(0, SEND // 8, pick, 0)
    lane = lax.broadcasted_iota(jnp.int32, (8, SEND), 1)
    rows = jnp.zeros((8, SEND), jnp.int32)
    for s in range(SEND):
        rows = jnp.where(lane == s, rows_ref[s], rows)
    chosen = jnp.zeros((8, SEND), F32)
    place, inside = rows // 128, rows % 128
    for chunk in range(ATOMS // 128):
        part = jnp.concatenate(
            [pos_ref[:, chunk * 128 : chunk * 128 + 128], jnp.zeros((5, 128), F32)], axis=0
        )
        found = jnp.take_along_axis(part, inside, axis=1)
        chosen = jnp.where(place == chunk, found, chosen)
    first = chosen.astype(BF16).astype(F32)
    second = (chosen - first).astype(BF16).astype(F32)
    third = (chosen - first) - second
    block[0:128, :] = mine[...].astype(BF16)
    block[128:144, :] = jnp.concatenate(
        [first[0:3], second[0:3], third[0:3], jnp.zeros((7, 128), F32)], axis=0
    ).astype(BF16)


def spread(c, own_ref, other_ref, basez, send_ref, whigh_ref, wlow_ref, table_ref):
    centre = jnp.concatenate([own_ref[...], other_ref[...]], axis=1)
    own = lax.broadcasted_iota(jnp.int32, (1, 2 * WC), 1) < WC
    charge = centre[0:1] * jnp.where(own, jnp.where(c == 1, -1.0, 1.0), 1.0)
    for d in range(2):
        base, frac = centre[1 + d : 2 + d], centre[4 + d : 5 + d]
        table_ref[40 * d : 40 * d + 40, :] = spline_table(base, spline_weights(frac), 40)
        table_ref[80 + 40 * d : 120 + 40 * d, :] = spline_table(base, spline_slopes(frac), 40)
    base, frac = centre[3:4], centre[6:7]
    for part, weights in enumerate((spline_weights(frac), spline_slopes(frac))):
        table = split(spline_table(base, weights, 144))
        high, low = split(dot3(basez, table, NN))
        whigh_ref[:, 1024 * part : 1024 * part + 1024] = high
        wlow_ref[:, 1024 * part : 1024 * part + 1024] = low
    wave = (whigh_ref[:, 0:1024], wlow_ref[:, 0:1024])
    along_y = table_ref[40:80, :] * charge
    gap = jnp.zeros((8, 2 * WC), F32)
    for row in range(0, ROWS, 2):
        pieces = []
        for part in range(6):
            shift = 3 * row + part
            pieces.append(along_y * table_ref[shift : shift + 1, :])
            if part % 3 == 2:
                pieces.append(gap)
        plane = split(jnp.concatenate(pieces, axis=0))
        waves = dot3(wave, plane, NT)
        for q in range(2):
            for h in range(2):
                send_ref[pl.ds(q * ROWS + row + h, 64, stride=SIDE), :] = waves[
                    64 * q : 64 * q + 64, 128 * h : 128 * h + 128
                ]


def folded(green_ref):
    first = green_ref[0:1, 0:128]
    lane = lax.broadcasted_iota(jnp.int32, (1, 128), 1)
    second = jnp.where(lane == 0, jnp.broadcast_to(green_ref[0:1, 128:129], (1, 128)), first)
    return jnp.concatenate([first, second], axis=1)


def screen(owner, recv_ref, greens, along_ref, across_ref, across_t_ref, send_ref):
    total = jnp.zeros((192, 768), F32)
    for pair in range(4):
        parts = [
            jnp.concatenate(
                [recv_ref[SIDE * (8 * a + 2 * pair + h) : SIDE * (8 * a + 2 * pair + h + 1), :] for a in range(8)], axis=0
            )
            for h in range(2)
        ]
        left = split(jnp.concatenate(parts, axis=1))
        right = tuple(along_ref[h, 256 * pair : 256 * pair + 256, :] for h in range(2))
        total = total + dot3(left, right, NN)
    stacked = split(jnp.concatenate([total[:, 256 * i : 256 * i + 256] for i in range(3)], axis=0))
    spectrum = dot3((across_ref[0], across_ref[1]), stacked, NN)
    row = lax.broadcasted_iota(jnp.int32, (M, M), 0)
    col = lax.broadcasted_iota(jnp.int32, (M, M), 1)
    gx, gy, gz = (folded(g) for g in greens)
    down = jnp.sum(jnp.where(row == col, gx, 0.0), axis=1, keepdims=True)
    lanes = lax.broadcasted_iota(jnp.int32, (1, M), 1)
    second = jnp.where(owner == 0, 128, owner)
    planes = []
    for q, wave in enumerate((owner, second)):
        level = jnp.sum(jnp.where(lanes == wave, gz, 0.0), axis=1, keepdims=True)
        planes.append(spectrum[256 * q : 256 * q + 256] / ((down + gy) + level))
    filtered = split(jnp.concatenate(planes, axis=0))
    space = dot3((across_t_ref[0], across_t_ref[1]), filtered, NN)
    space = split(jnp.concatenate([space[192 * i : 192 * i + 192] for i in range(3)], axis=1))
    for pair in range(4):
        right = tuple(along_ref[h, 256 * pair : 256 * pair + 256, :] for h in range(2))
        out = dot3(space, right, NT)
        for h in range(2):
            for a in range(8):
                to = SIDE * (8 * a + 2 * pair + h)
                send_ref[to : to + SIDE, :] = out[SIDE * a : SIDE * a + SIDE, 128 * h : 128 * h + 128]


def gather_centres(recv_ref, whigh_ref, wlow_ref, table_ref):
    sums = [jnp.zeros((8, 2 * WC), F32) for _ in range(4)]
    wave = (whigh_ref[...], wlow_ref[...])
    for row in range(ROWS):
        field = jnp.concatenate(
            [recv_ref[pl.ds(q * ROWS + row, 64, stride=SIDE), :] for q in range(2)], axis=0
        )
        local = dot3(split(field.T), wave, NN)
        for part in range(3):
            shift = 3 * row + part
            if shift >= 35:
                continue
            flat, steep, upright = 0.0, 0.0, 0.0
            for h in range(5):
                at = 40 * part + 8 * h
                value, slope = local[at : at + 8, 0:1024], local[at : at + 8, 1024:2048]
                weight = table_ref[40 + 8 * h : 48 + 8 * h, :]
                flat = flat + value * weight
                steep = steep + value * table_ref[120 + 8 * h : 128 + 8 * h, :]
                upright = upright + slope * weight
            weight = table_ref[shift : shift + 1, :]
            sums[0] = sums[0] + flat * weight
            sums[1] = sums[1] + flat * table_ref[80 + shift : 81 + shift, :]
            sums[2] = sums[2] + steep * weight
            sums[3] = sums[3] + upright * weight
    return jnp.concatenate([jnp.sum(s, axis=0, keepdims=True) for s in sums], axis=0)


FIRST = 14


def kernel(index_ref, rows_ref, pairs_ref, feat_ref, pos_ref, wproj_ref, wradial_ref, whidden_ref, wout_ref,
           charge_ref, base_ref, frac_ref, gx_ref, gy_ref, gz_ref, basez_ref, along_any, across_any, acrosst_any,
           atom_ref, centre_ref,
           along_ref, across_ref, acrosst_ref, wide, mine, near_ref, own_ref, other_ref,
           send1, recv1, send2, recv2, whigh, wlow, splines, half, got,
           table, own_t, place, disp, dist, basis, slope, rows, score, dscore, wrad, wh, wht, wout,
           const_sem, pack_sem, near_sem, far_sem, there_sem, back_sem, last_sem):
    a, b, c = position()
    me = a * 8 + b
    partner = (a, b, (c + 1) % 2)

    def fellow(step):
        to = (me + step) % 64
        return to, (to // 8, to % 8, c)

    loads = [
        pltpu.make_async_copy(src, dst, const_sem.at[i])
        for i, (src, dst) in enumerate(
            ((along_any, along_ref), (across_any, across_ref), (acrosst_any, acrosst_ref))
        )
    ]
    for load in loads:
        load.start()
    barrier = pltpu.get_barrier_semaphore()

    def greet(step, _):
        pl.semaphore_signal(barrier, inc=1, device_id=fellow(step)[1], device_id_type=MESH)
        return 0

    lax.fori_loop(1, 64, greet, 0)
    for dy in (-1, 0, 1):
        pl.semaphore_signal(barrier, inc=1, device_id=around(a, b, c, (0, dy, 1)), device_id_type=MESH)
    own = block_of((0, 0, 0))
    own_ref[0:1, :] = charge_ref[...]
    own_ref[1:4, :] = base_ref[...].astype(F32)
    own_ref[4:7, :] = frac_ref[...]
    own_ref[7:8, :] = jnp.zeros((1, WC), F32)
    offer(rows_ref, feat_ref, pos_ref, wide, mine, near_ref.at[own])
    pl.semaphore_wait(barrier, 66)
    pack = pltpu.make_async_remote_copy(
        own_ref, other_ref, pack_sem.at[0], pack_sem.at[1], device_id=partner, device_id_type=MESH
    )
    pack.start()
    for step in ((0, 0, 1), (0, -1, 0), (0, 1, 0), (0, -1, 1), (0, 1, 1)):
        back = block_of((0, -step[1], step[2]))
        pltpu.make_async_remote_copy(
            near_ref.at[own], near_ref.at[back], near_sem.at[0], near_sem.at[1],
            device_id=around(a, b, c, step), device_id_type=MESH,
        ).start()

    radial = 0.5 * wradial_ref[...]
    high = radial.astype(BF16).astype(F32)
    wrad[...] = jnp.concatenate([high, high, radial - high, jnp.zeros((104, 128), F32)], axis=0).T.astype(BF16)
    hidden = 0.5 * whidden_ref[...].astype(F32)
    wh[...] = hidden.astype(BF16)
    wht[...] = hidden.T.astype(BF16)
    wout[...] = jnp.broadcast_to(wout_ref[...], (128, 128)).T

    pltpu.make_async_remote_copy(
        near_ref.at[pl.ds(0, 5)], near_ref.at[pl.ds(0, 5)], near_sem.at[0], near_sem.at[1],
        device_id=partner, device_id_type=MESH,
    ).wait()
    for dx in (1, -1):
        pltpu.make_async_remote_copy(
            near_ref.at[pl.ds(6, 6)], near_ref.at[pl.ds(6 - 6 * dx, 6)], far_sem.at[0], far_sem.at[1],
            device_id=around(a, b, c, (dx, 0, 0)), device_id_type=MESH,
        ).start()
    pack.wait()
    spread(c, own_ref, other_ref, (basez_ref[0, c], basez_ref[1, c]), send1, whigh, wlow, splines)

    def post(x_ref, o_ref, sems):
        def send(step, _):
            to, device = fellow(step)
            pltpu.make_async_remote_copy(
                x_ref.at[pl.ds(pl.multiple_of(to * SIDE, SIDE), SIDE), :],
                o_ref.at[pl.ds(pl.multiple_of(me * SIDE, SIDE), SIDE), :],
                sems.at[0], sems.at[1], device_id=device, device_id_type=MESH,
            ).start()
            return 0

        lax.fori_loop(1, 64, send, 0)
        mine = pl.ds(pl.multiple_of(me * SIDE, SIDE), SIDE)
        o_ref[mine, :] = x_ref[mine, :]

    def collect(x_ref, o_ref, sems):
        pltpu.make_async_remote_copy(
            x_ref.at[pl.ds(0, 63 * SIDE), :], o_ref.at[pl.ds(0, 63 * SIDE), :], sems.at[0], sems.at[1],
            device_id=partner, device_id_type=MESH,
        ).wait()

    post(send1, recv1, there_sem)
    pltpu.make_async_remote_copy(
        near_ref.at[pl.ds(0, 12)], near_ref.at[pl.ds(0, 12)], far_sem.at[0], far_sem.at[1],
        device_id=partner, device_id_type=MESH,
    ).wait()
    pair_setup(feat_ref, near_ref, pos_ref, wproj_ref, pairs_ref, table, own_t, place, disp, dist, basis, slope)
    chunks = NEIGH * ATOMS // CHUNK
    pair_chunks(0, FIRST, index_ref, table, own_t, basis, slope, wrad, wh, wht, wout, rows, score, dscore)
    for load in loads:
        load.wait()
    collect(send1, recv1, there_sem)
    screen(me * 2 + c, recv1, (gx_ref, gy_ref, gz_ref), along_ref, across_ref, acrosst_ref, send2)
    post(send2, recv2, back_sem)
    pair_chunks(FIRST, chunks, index_ref, table, own_t, basis, slope, wrad, wh, wht, wout, rows, score, dscore)
    pair_finish(disp, dist, score, dscore, atom_ref)
    collect(send2, recv2, back_sem)
    sums = gather_centres(recv2, whigh, wlow, splines)
    half[0:4, :] = sums[:, WC:]
    half[4:8, :] = jnp.zeros((4, WC), F32)
    last = pltpu.make_async_remote_copy(
        half, got, last_sem.at[0], last_sem.at[1], device_id=partner, device_id_type=MESH
    )
    last.start()
    ours = sums[:, :WC] * jnp.where(c == 1, -1.0, 1.0)
    last.wait()
    whole = ours + got[0:4, :]
    centre_ref[...] = jnp.concatenate([whole[0:1], whole[1:4] * charge_ref[...]], axis=0)


def shape(*dims, dtype=F32):
    return jax.ShapeDtypeStruct(dims, dtype)


DMA = pltpu.SemaphoreType.DMA
SCRATCH = [
    VMEM((2, 1024, 768), BF16), VMEM((2, 512, 576), BF16), VMEM((2, 576, 512), BF16),
    VMEM((ATOMS, 128), F32), VMEM((SEND, 128), F32), VMEM((18, BLOCK, 128), BF16), VMEM((8, WC), F32), VMEM((8, WC), F32),
    VMEM((64 * SIDE, 128), F32), VMEM((64 * SIDE, 128), F32), VMEM((64 * SIDE, 128), F32), VMEM((64 * SIDE, 128), F32),
    VMEM((128, 2048), BF16), VMEM((128, 2048), BF16), VMEM((160, 1024), F32), VMEM((8, WC), F32), VMEM((8, WC), F32),
    VMEM((4480, 128), F32), VMEM((128, ATOMS), F32), VMEM((120, 128), F32), VMEM((48, ATOMS), F32),
    VMEM((16, ATOMS), F32), VMEM((1024, 128), F32), VMEM((1024, 128), F32),
    (VMEM((CHUNK, 128), F32), VMEM((CHUNK, 128), F32)), VMEM((16, ATOMS), F32), VMEM((16, ATOMS), F32),
    VMEM((128, 128), BF16), VMEM((128, 128), BF16), VMEM((128, 128), BF16), VMEM((128, 128), F32),
    DMA((3,)), DMA((2,)), DMA((2,)), DMA((2,)), DMA((2,)), DMA((2,)), DMA((2,)),
]


def on_device(base_z, along, across, across_t,
    atom_feat, atom_pos, pair_list, halo_rows, w_proj, w_radial, w_hidden, w_out,
    centre_charge, centre_base, centre_frac, green_x, green_y, green_z,
):
    args = (
        pair_list.reshape(-1), halo_rows, pair_list, atom_feat, atom_pos, w_proj, w_radial, w_hidden, w_out[None],
        centre_charge[None], centre_base, centre_frac, green_x[None], green_y[None], green_z[None],
        base_z, along, across, across_t,
    )
    spec = pl.BlockSpec(memory_space=VMEM)
    scalar = pl.BlockSpec(memory_space=pltpu.SMEM)
    still = pl.BlockSpec(memory_space=pl.ANY)
    return tuple(
        pl.pallas_call(
            kernel,
            out_shape=[shape(4, ATOMS), shape(4, WC)],
            in_specs=[scalar] * 2 + [spec] * 14 + [still] * 3,
            out_specs=[spec, spec],
            scratch_shapes=SCRATCH,
            compiler_params=pltpu.CompilerParams(
                vmem_limit_bytes=56 << 20, collective_id=1, has_side_effects=True
            ),
        )(*args)
    )


def solution(mesh):
    device = P(("gx", "gy", "gz"))
    late = P(None, ("gx", "gy", "gz"))
    tables = [jnp.asarray(t) for t in constants()]

    def run(*args):
        return jax.shard_map(
            on_device,
            mesh=mesh,
            in_specs=(P(), P(), P(), P(),
                P(("gx", "gy", "gz"), None), late, late, device,
                P(), P(), P(), P(), device, late, late, P(), P(), P(),
            ),
            out_specs=(late, late),
            check_vma=False,
        )(*tables, *args)

    return run
```

```python
import functools

import jax
import jax.numpy as jnp
import numpy as np
from jax import lax
from jax.experimental import pallas as pl
from jax.experimental.pallas import tpu as pltpu
from jax.sharding import PartitionSpec as P

M = 256
ATOMS = 1024
SEND = 128
WC = 512
NEIGH = 16
BLOCK = 144
MESH = pl.DeviceIdType.MESH
VMEM = pltpu.VMEM
F32 = jnp.float32
BF16 = jnp.bfloat16
ROWS = 12
SIDE = 24
NN = (((1,), (0,)), ((), ()))
NT = (((1,), (1,)), ((), ()))


def real_basis(index, points):
    wave = np.where(index <= 128, index, index - 128)
    scale = np.where((index == 0) | (index == 128), 1.0 / 16.0, np.sqrt(2.0) / 16.0)
    angle = 2.0 * np.pi * ((wave[:, None] * points[None, :]) % M) / M
    return scale[:, None] * np.where((index <= 128)[:, None], np.cos(angle), np.sin(angle))


def halves(value):
    value = np.asarray(value, np.float32)
    high = value.astype(jnp.bfloat16)
    low = (value - high.astype(np.float32)).astype(jnp.bfloat16)
    return np.stack([high, low])


def constants():
    waves = np.arange(M)
    base_z = np.zeros((2, 128, 144))
    for parity in range(2):
        owner = 2 * np.arange(64) + parity
        index = np.concatenate([owner, owner + 128])
        base_z[parity] = real_basis(index, np.arange(144) - 1)
    along = np.zeros((8, 128, 768))
    for brick in range(8):
        points = (32 * brick + np.arange(35) - 1) % M
        table = real_basis(waves, points)
        for part in range(3):
            along[brick, 40 * part : 40 * part + 35, 256 * part : 256 * part + 256] = table.T
    across = np.zeros((2, 256, 3, 8, 2, ROWS))
    for brick in range(8):
        for part in range(3):
            for row in range(ROWS):
                shift = 3 * row + part
                if shift < 35:
                    value = real_basis(waves, np.array([(32 * brick + shift - 1) % M]))[:, 0]
                    across[0, :, part, brick, 0, row] = value
                    across[1, :, part, brick, 1, row] = value
    across = across.reshape(512, 576)
    return halves(base_z), halves(along.reshape(1024, 768)), halves(across), halves(across.T)


def split(value):
    high = value.astype(BF16)
    return high, (value - high.astype(F32)).astype(BF16)


def dot(a, b, dims):
    return lax.dot_general(a, b, dims, preferred_element_type=F32)


def dot3(a, b, dims):
    return dot(a[0], b[0], dims) + (dot(a[1], b[0], dims) + dot(a[0], b[1], dims))


def position():
    return lax.axis_index("gx"), lax.axis_index("gy"), lax.axis_index("gz")


def spline_weights(frac):
    rest = 1.0 - frac
    square = frac * frac
    cube = square * frac
    return (
        rest * rest * rest / 6.0,
        (3.0 * cube - 6.0 * square + 4.0) / 6.0,
        (-3.0 * cube + 3.0 * square + 3.0 * frac + 1.0) / 6.0,
        cube / 6.0,
    )


def spline_slopes(frac):
    rest = 1.0 - frac
    square = frac * frac
    return (
        -0.5 * rest * rest,
        (3.0 * square - 4.0 * frac) / 2.0,
        (-3.0 * square + 2.0 * frac + 1.0) / 2.0,
        0.5 * square,
    )


def spline_table(base, weights, length):
    points = lax.broadcasted_iota(jnp.int32, (length, base.shape[1]), 0).astype(F32)
    away = points - base
    table = jnp.where(away == 0.0, weights[0], 0.0)
    for shift in range(1, 4):
        table = jnp.where(away == float(shift), weights[shift], table)
    return table


def around(a, b, c, step):
    return (a + step[0] + 8) % 8, (b + step[1] + 8) % 8, (c + step[2]) % 2


def block_of(step):
    return (step[0] + 1) * 6 + (step[1] + 1) * 2 + abs(step[2])


STEPS = [
    (dx, dy, dz)
    for dx in (-1, 0, 1)
    for dy in (-1, 0, 1)
    for dz in (0, 1)
    if (dx, dy, dz) != (0, 0, 0)
]


CHUNK = 512
TURNS, EACH = 3, 18


def pair_setup(feat_ref, near_ref, pos_ref, wproj_ref, pairs_ref, table, own_t, place, disp, dist, basis, slope):
    weight = wproj_ref[...]
    for chunk in range(8):
        rows = 0.5 * dot(feat_ref[128 * chunk : 128 * chunk + 128, :], weight, NN)
        table[128 * chunk : 128 * chunk + 128, :] = rows
        own_t[:, 128 * chunk : 128 * chunk + 128] = rows.T
        for d in range(3):
            place[40 * d + chunk : 40 * d + chunk + 1, :] = pos_ref[d : d + 1, 128 * chunk : 128 * chunk + 128]
    for dx in range(3):
        for dy in range(3):
            for dz in range(2):
                block = dx * 6 + dy * 2 + dz
                rows = 0.5 * dot(near_ref[block, 0:128, :], weight, NN)
                parts = near_ref[block, 128:144, :].astype(F32)
                where = (parts[0:3] + parts[3:6]) + parts[6:9]
                for sz in ((0,), (-1, 1))[dz]:
                    e = dx * 9 + dy * 3 + sz + 1
                    table[1024 + 128 * e : 1152 + 128 * e, :] = rows
                    for d, shift in enumerate((dx - 1, dy - 1, sz)):
                        place[40 * d + 8 + e : 40 * d + 9 + e, :] = where[d : d + 1] + 4.0 * shift

    def locate(tile, _):
        lanes = pl.ds(pl.multiple_of(tile * 128, 128), 128)
        for half in range(2):
            index = pairs_ref[8 * half : 8 * half + 8, lanes]
            chunk, inside = index // 128, index % 128
            found = [jnp.zeros((8, 128), F32)] * 3
            for k in range(35):
                here = chunk == k
                for d in range(3):
                    row = jnp.broadcast_to(place[40 * d + k : 40 * d + k + 1, :], (8, 128))
                    found[d] = jnp.where(here, jnp.take_along_axis(row, inside, axis=1), found[d])
            square = 0.0
            for d in range(3):
                away = found[d] - pos_ref[d : d + 1, lanes]
                disp[16 * d + 8 * half : 16 * d + 8 * half + 8, lanes] = away
                square = square + away * away
            length = jnp.sqrt(square + 0.25)
            dist[8 * half : 8 * half + 8, lanes] = length
            inverse = 1.0 / length
            theta = length * (np.pi / 12.0)
            sine, cosine = jnp.sin(theta), jnp.cos(theta)
            twice = 2.0 * cosine
            s0, s1, c0, c1 = 0.0, sine, 1.0, cosine
            for m in range(1, 9):
                base = s1 * inverse
                at = pl.ds(128 * tile + 64 * half + m - 1, 8, stride=8)
                basis[at, :] = base
                slope[at, :] = (float(m * np.pi / 12.0) * c1 - base) * inverse
                s0, s1 = s1, twice * s1 - s0
                c0, c1 = c1, twice * c1 - c0
        return 0

    lax.fori_loop(0, 8, locate, 0)


def pair_chunks(first, last, index_ref, table, own_t, basis, slope, wrad_ref, wh_ref, wht_ref, wout_ref,
                rows, score, dscore, post):
    per = ATOMS // CHUNK
    wout = jnp.concatenate([wout_ref[...]] * (CHUNK // 128), axis=1)

    def fetch(step, into):
        base = step * CHUNK
        for r in range(CHUNK):
            into[r : r + 1, :] = table[pl.ds(index_ref[base + r], 1), :]

    def work(step, rows):
        slot = step // per
        start = pl.multiple_of((step % per) * CHUNK, CHUNK)
        lanes = pl.ds(start, CHUNK)

        def stack(table):
            tile = (step % per) * (CHUNK // 128)
            value = jnp.concatenate(
                [table[pl.ds(pl.multiple_of(128 * (tile + t) + 8 * slot, 8), 8), :] for t in range(CHUNK // 128)],
                axis=1,
            )
            high = value.astype(BF16).astype(F32)
            return jnp.concatenate([high, value - high, high], axis=0).astype(BF16)

        radial = dot(wrad_ref[:, 0:24], stack(basis), NN)
        grad_radial = dot(wrad_ref[:, 0:24], stack(slope), NN)
        half = (rows[...].T + own_t[:, lanes]) + radial
        tan = jnp.tanh(half)
        up = 1.0 + tan
        hidden = (half * up).astype(BF16)
        inner = dot(wht_ref[...], hidden, NN)
        tan2 = jnp.tanh(inner)
        weighted = wout * (1.0 + tan2)
        score[pl.ds(slot, 1), lanes] = jnp.sum(weighted * inner, axis=0, keepdims=True)
        back = (weighted * (1.0 + inner * (1.0 - tan2))).astype(BF16)
        grad = dot(wh_ref[...], back, NN)
        bend = up * (1.0 + half * (1.0 - tan))
        dscore[pl.ds(slot, 1), lanes] = jnp.sum(grad * bend * grad_radial, axis=0, keepdims=True)

    fetch(first, rows[0])

    def one(turn, _):
        step = first + 2 * turn

        @pl.when(turn < TURNS)
        def _():
            for i in range(EACH):
                post(64 - TURNS * EACH + turn * EACH + i)

        fetch(step + 1, rows[1])
        work(step, rows[0])
        fetch(jnp.minimum(step + 2, last - 1), rows[0])
        work(step + 1, rows[1])
        return 0

    lax.fori_loop(0, (last - first) // 2, one, 0)


def pair_finish(disp, dist, score, dscore, out_ref):
    length = dist[...]
    env = jnp.exp(-((length / 6.0) * (length / 6.0)))
    energy = env * score[...]
    push = (env * dscore[...] - 2.0 * length / 36.0 * energy) / length
    out_ref[0:1, :] = jnp.sum(energy, axis=0, keepdims=True)
    for d in range(3):
        out_ref[1 + d : 2 + d, :] = jnp.sum(push * disp[16 * d : 16 * d + 16, :], axis=0, keepdims=True)


def offer(rows_ref, feat_ref, pos_ref, wide, mine, block):
    wide[...] = feat_ref[...].astype(F32)

    def pick(group, _):
        base = group * 8
        for s in range(8):
            mine[pl.ds(base + s, 1), :] = wide[pl.ds(rows_ref[base + s], 1), :]
        return 0

    lax.fori_loop(0, SEND // 8, pick, 0)
    lane = lax.broadcasted_iota(jnp.int32, (8, SEND), 1)
    rows = jnp.zeros((8, SEND), jnp.int32)
    for s in range(SEND):
        rows = jnp.where(lane == s, rows_ref[s], rows)
    chosen = jnp.zeros((8, SEND), F32)
    place, inside = rows // 128, rows % 128
    for chunk in range(ATOMS // 128):
        part = jnp.concatenate(
            [pos_ref[:, chunk * 128 : chunk * 128 + 128], jnp.zeros((5, 128), F32)], axis=0
        )
        found = jnp.take_along_axis(part, inside, axis=1)
        chosen = jnp.where(place == chunk, found, chosen)
    first = chosen.astype(BF16).astype(F32)
    second = (chosen - first).astype(BF16).astype(F32)
    third = (chosen - first) - second
    block[0:128, :] = mine[...].astype(BF16)
    block[128:144, :] = jnp.concatenate(
        [first[0:3], second[0:3], third[0:3], jnp.zeros((7, 128), F32)], axis=0
    ).astype(BF16)


def spread(c, which, centre_ref, basez, send_ref, wave_ref, table_ref):
    centre = centre_ref[...]
    lanes = slice(WC * which, WC * which + WC)
    charge = centre[0:1]
    if which == 0:
        charge = charge * jnp.where(c == 1, -1.0, 1.0)
    for d in range(2):
        base, frac = centre[1 + d : 2 + d], centre[4 + d : 5 + d]
        table_ref[40 * d : 40 * d + 40, lanes] = spline_table(base, spline_weights(frac), 40)
        table_ref[80 + 40 * d : 120 + 40 * d, lanes] = spline_table(base, spline_slopes(frac), 40)
    base, frac = centre[3:4], centre[6:7]
    for part, weights in enumerate((spline_weights(frac), spline_slopes(frac))):
        table = split(spline_table(base, weights, 144))
        high, low = split(dot3(basez, table, NN))
        if part == 0:
            wave = jnp.concatenate([high, low, high], axis=1)
        for tile in range(4):
            at = slice(128 * part, 128 * part + 128)
            piece = slice(128 * tile, 128 * tile + 128)
            wave_ref[4 * which + tile, 0:128, at] = high[:, piece]
            wave_ref[4 * which + tile, 128:256, at] = high[:, piece]
            wave_ref[4 * which + tile, 256:384, at] = low[:, piece]
    along_y = table_ref[40:80, lanes] * charge
    gap = jnp.zeros((8, WC), F32)
    for row in range(0, ROWS, 2):
        pieces = []
        for part in range(6):
            shift = 3 * row + part
            pieces.append(along_y * table_ref[shift : shift + 1, lanes])
            if part % 3 == 2:
                pieces.append(gap)
        high, low = split(jnp.concatenate(pieces, axis=0))
        waves = dot(wave, jnp.concatenate([high, high, low], axis=1), NT)
        for q in range(2):
            for h in range(2):
                at = pl.ds(q * ROWS + row + h, 64, stride=SIDE)
                value = waves[64 * q : 64 * q + 64, 128 * h : 128 * h + 128]
                send_ref[at, :] = value if which == 0 else send_ref[at, :] + value


def folded(green_ref):
    first = green_ref[0:1, 0:128]
    lane = lax.broadcasted_iota(jnp.int32, (1, 128), 1)
    second = jnp.where(lane == 0, jnp.broadcast_to(green_ref[0:1, 128:129], (1, 128)), first)
    return jnp.concatenate([first, second], axis=1)


def screen(owner, recv_ref, greens, along_ref, across_ref, across_t_ref, send_ref):
    parts = [
        jnp.concatenate([recv_ref[SIDE * (8 * a + b) : SIDE * (8 * a + b + 1), :] for a in range(8)], axis=0)
        for b in range(8)
    ]
    along = (along_ref[0], along_ref[1])
    total = dot3(split(jnp.concatenate(parts, axis=1)), along, NN)
    stacked = split(jnp.concatenate([total[:, 256 * i : 256 * i + 256] for i in range(3)], axis=0))
    spectrum = dot3((across_ref[0], across_ref[1]), stacked, NN)
    row = lax.broadcasted_iota(jnp.int32, (M, M), 0)
    col = lax.broadcasted_iota(jnp.int32, (M, M), 1)
    gx, gy, gz = (folded(g) for g in greens)
    down = jnp.sum(jnp.where(row == col, gx, 0.0), axis=1, keepdims=True)
    lanes = lax.broadcasted_iota(jnp.int32, (1, M), 1)
    second = jnp.where(owner == 0, 128, owner)
    planes = []
    for q, wave in enumerate((owner, second)):
        level = jnp.sum(jnp.where(lanes == wave, gz, 0.0), axis=1, keepdims=True)
        planes.append(spectrum[256 * q : 256 * q + 256] / ((down + gy) + level))
    filtered = split(jnp.concatenate(planes, axis=0))
    space = dot3((across_t_ref[0], across_t_ref[1]), filtered, NN)
    space = split(jnp.concatenate([space[192 * i : 192 * i + 192] for i in range(3)], axis=1))
    out = dot3(space, along, NT)
    for a in range(8):
        for b in range(8):
            to = SIDE * (8 * a + b)
            send_ref[to : to + SIDE, :] = out[SIDE * a : SIDE * a + SIDE, 128 * b : 128 * b + 128]


def turn_fields(recv_ref, field_ref):
    for row in range(ROWS):
        field = jnp.concatenate(
            [recv_ref[pl.ds(q * ROWS + row, 64, stride=SIDE), :] for q in range(2)], axis=0
        )
        high, low = split(field.T)
        field_ref[128 * row : 128 * row + 128, :] = jnp.concatenate([high, low, high], axis=1)


def gather_centres(which, field_ref, wave_ref, table_ref, sum_ref):
    def one(tile, _):
        tile = tile + 4 * which
        lanes = pl.ds(pl.multiple_of(tile * 128, 128), 128)
        local = dot(field_ref[...], wave_ref[tile], NN)
        table = table_ref[:, lanes]
        sums = [jnp.zeros((8, 128), F32) for _ in range(4)]
        for shift in range(35):
            flat, steep, upright = 0.0, 0.0, 0.0
            for h in range(5):
                at = 128 * (shift // 3) + 40 * (shift % 3) + 8 * h
                value, slope = local[at : at + 8, 0:128], local[at : at + 8, 128:256]
                weight = table[40 + 8 * h : 48 + 8 * h]
                flat = flat + value * weight
                steep = steep + value * table[120 + 8 * h : 128 + 8 * h]
                upright = upright + slope * weight
            weight = table[shift : shift + 1]
            sums[0] = sums[0] + flat * weight
            sums[1] = sums[1] + flat * table[80 + shift : 81 + shift]
            sums[2] = sums[2] + steep * weight
            sums[3] = sums[3] + upright * weight
        for r in range(4):
            sum_ref[r : r + 1, lanes] = jnp.sum(sums[r], axis=0, keepdims=True)
        return 0

    lax.fori_loop(0, 4, one, 0)


FIRST = 16


def kernel(rows_ref, pairs_ref, feat_ref, pos_ref, wproj_ref, wradial_ref, whidden_ref, wout_ref,
           charge_ref, base_ref, frac_ref, gx_ref, gy_ref, gz_ref, basez_ref, along_any, across_any, acrosst_any,
           atom_ref, centre_ref,
           along_ref, across_ref, acrosst_ref, wide, mine, near_ref, own_ref, other_ref,
           index_ref, send1, recv1, send2, recv2, wave, splines, fields, sums, half, got,
           table, own_t, place, disp, dist, basis, slope, rows, score, dscore, wrad, wh, wht, wout,
           const_sem, index_sem, pack_sem, near_sem, far_sem, there_sem, back_sem, last_sem):
    a, b, c = position()
    me = a * 8 + b
    partner = (a, b, (c + 1) % 2)

    def fellow(step):
        to = (me + step) % 64
        return to, (to // 8, to % 8, c)

    loads = [
        pltpu.make_async_copy(src, dst, const_sem.at[i])
        for i, (src, dst) in enumerate(
            ((along_any, along_ref), (across_any, across_ref), (acrosst_any, acrosst_ref))
        )
    ]
    for load in loads:
        load.start()
    lists = [
        pltpu.make_async_copy(pairs_ref.at[k], index_ref.at[pl.ds(k * ATOMS, ATOMS)], index_sem.at[k]) for k in range(NEIGH)
    ]
    for copy in lists:
        copy.start()
    barrier = pltpu.get_barrier_semaphore()

    def greet(step, _):
        pl.semaphore_signal(barrier, inc=1, device_id=fellow(step)[1], device_id_type=MESH)
        return 0

    lax.fori_loop(1, 64, greet, 0)
    for dy in (-1, 0, 1):
        pl.semaphore_signal(barrier, inc=1, device_id=around(a, b, c, (0, dy, 1)), device_id_type=MESH)
    own = block_of((0, 0, 0))
    own_ref[0:1, :] = charge_ref[...]
    own_ref[1:4, :] = base_ref[...].astype(F32)
    own_ref[4:7, :] = frac_ref[...]
    own_ref[7:8, :] = jnp.zeros((1, WC), F32)
    offer(rows_ref, feat_ref, pos_ref, wide, mine, near_ref.at[own])
    radial = 0.5 * wradial_ref[...]
    high = radial.astype(BF16).astype(F32)
    wrad[...] = jnp.concatenate([high, high, radial - high, jnp.zeros((104, 128), F32)], axis=0).T.astype(BF16)
    hidden = 0.5 * whidden_ref[...].astype(F32)
    wh[...] = hidden.astype(BF16)
    wht[...] = hidden.T.astype(BF16)
    wout[...] = jnp.broadcast_to(wout_ref[...], (128, 128)).T
    basez = (basez_ref[0, c], basez_ref[1, c])
    spread(c, 0, own_ref, basez, send1, wave, splines)
    pl.semaphore_wait(barrier, 66)
    pack = pltpu.make_async_remote_copy(
        own_ref, other_ref, pack_sem.at[0], pack_sem.at[1], device_id=partner, device_id_type=MESH
    )
    pack.start()
    for step in ((0, 0, 1), (0, -1, 0), (0, 1, 0), (0, -1, 1), (0, 1, 1)):
        back = block_of((0, -step[1], step[2]))
        pltpu.make_async_remote_copy(
            near_ref.at[own], near_ref.at[back], near_sem.at[0], near_sem.at[1],
            device_id=around(a, b, c, step), device_id_type=MESH,
        ).start()

    pltpu.make_async_remote_copy(
        near_ref.at[pl.ds(0, 5)], near_ref.at[pl.ds(0, 5)], near_sem.at[0], near_sem.at[1],
        device_id=partner, device_id_type=MESH,
    ).wait()
    for dx in (1, -1):
        pltpu.make_async_remote_copy(
            near_ref.at[pl.ds(6, 6)], near_ref.at[pl.ds(6 - 6 * dx, 6)], far_sem.at[0], far_sem.at[1],
            device_id=around(a, b, c, (dx, 0, 0)), device_id_type=MESH,
        ).start()
    pack.wait()
    spread(c, 1, other_ref, basez, send1, wave, splines)

    def sender(x_ref, o_ref, sems):
        def send(step):
            to, device = fellow(step)
            pltpu.make_async_remote_copy(
                x_ref.at[pl.ds(pl.multiple_of(to * SIDE, SIDE), SIDE), :],
                o_ref.at[pl.ds(pl.multiple_of(me * SIDE, SIDE), SIDE), :],
                sems.at[0], sems.at[1], device_id=device, device_id_type=MESH,
            ).start()

        def early(step, _):
            send(step)
            return 0

        lax.fori_loop(1, 64 - TURNS * EACH, early, 0)
        mine = pl.ds(pl.multiple_of(me * SIDE, SIDE), SIDE)
        o_ref[mine, :] = x_ref[mine, :]
        return send

    def collect(x_ref, o_ref, sems):
        pltpu.make_async_remote_copy(
            x_ref.at[pl.ds(0, 63 * SIDE), :], o_ref.at[pl.ds(0, 63 * SIDE), :], sems.at[0], sems.at[1],
            device_id=partner, device_id_type=MESH,
        ).wait()

    post = sender(send1, recv1, there_sem)
    pltpu.make_async_remote_copy(
        near_ref.at[pl.ds(0, 12)], near_ref.at[pl.ds(0, 12)], far_sem.at[0], far_sem.at[1],
        device_id=partner, device_id_type=MESH,
    ).wait()
    pair_setup(feat_ref, near_ref, pos_ref, wproj_ref, pairs_ref, table, own_t, place, disp, dist, basis, slope)
    chunks = NEIGH * ATOMS // CHUNK
    for copy in lists:
        copy.wait()
    pair_chunks(0, FIRST, index_ref, table, own_t, basis, slope, wrad, wh, wht, wout, rows, score, dscore, post)
    for load in loads:
        load.wait()
    collect(send1, recv1, there_sem)
    screen(me * 2 + c, recv1, (gx_ref, gy_ref, gz_ref), along_ref, across_ref, acrosst_ref, send2)
    post = sender(send2, recv2, back_sem)
    pair_chunks(FIRST, chunks, index_ref, table, own_t, basis, slope, wrad, wh, wht, wout, rows, score, dscore, post)
    pair_finish(disp, dist, score, dscore, atom_ref)
    collect(send2, recv2, back_sem)
    turn_fields(recv2, fields)
    gather_centres(1, fields, wave, splines, sums)
    half[0:4, :] = sums[:, WC:]
    half[4:8, :] = jnp.zeros((4, WC), F32)
    last = pltpu.make_async_remote_copy(
        half, got, last_sem.at[0], last_sem.at[1], device_id=partner, device_id_type=MESH
    )
    last.start()
    gather_centres(0, fields, wave, splines, sums)
    ours = sums[:, :WC] * jnp.where(c == 1, -1.0, 1.0)
    last.wait()
    centre_ref[...] = ours + got[0:4, :]


def scale_kernel(atom_ref, centre_ref, charge_ref, atom_out_ref, centre_out_ref):
    atom_out_ref[0:1, :] = 0.5 * atom_ref[0:1, :]
    atom_out_ref[1:4, :] = atom_ref[1:4, :]
    centre_out_ref[0:1, :] = centre_ref[0:1, :]
    centre_out_ref[1:4, :] = centre_ref[1:4, :] * charge_ref[...]


def shape(*dims, dtype=F32):
    return jax.ShapeDtypeStruct(dims, dtype)


DMA = pltpu.SemaphoreType.DMA
SCRATCH = [
    VMEM((2, 1024, 768), BF16), VMEM((2, 512, 576), BF16), VMEM((2, 576, 512), BF16),
    VMEM((ATOMS, 128), F32), VMEM((SEND, 128), F32), VMEM((18, BLOCK, 128), BF16), VMEM((8, WC), F32), VMEM((8, WC), F32),
    pltpu.SMEM((NEIGH * ATOMS,), jnp.int32),
    VMEM((64 * SIDE, 128), F32), VMEM((64 * SIDE, 128), F32), VMEM((64 * SIDE, 128), F32), VMEM((64 * SIDE, 128), F32),
    VMEM((8, 384, 256), BF16), VMEM((160, 1024), F32), VMEM((128 * ROWS, 384), BF16), VMEM((4, 1024), F32), VMEM((8, WC), F32), VMEM((8, WC), F32),
    VMEM((4480, 128), F32), VMEM((128, ATOMS), F32), VMEM((120, 128), F32), VMEM((48, ATOMS), F32),
    VMEM((16, ATOMS), F32), VMEM((1024, 128), F32), VMEM((1024, 128), F32),
    (VMEM((CHUNK, 128), F32), VMEM((CHUNK, 128), F32)), VMEM((16, ATOMS), F32), VMEM((16, ATOMS), F32),
    VMEM((128, 128), BF16), VMEM((128, 128), BF16), VMEM((128, 128), BF16), VMEM((128, 128), F32),
    DMA((3,)), DMA((NEIGH,)), DMA((2,)), DMA((2,)), DMA((2,)), DMA((2,)), DMA((2,)), DMA((2,)),
]


def on_device(base_z, along, across, across_t,
    atom_feat, atom_pos, pair_list, halo_rows, w_proj, w_radial, w_hidden, w_out,
    centre_charge, centre_base, centre_frac, green_x, green_y, green_z,
):
    args = (
        halo_rows, pair_list, atom_feat, atom_pos, w_proj, w_radial, w_hidden, w_out[None],
        centre_charge[None], centre_base, centre_frac, green_x[None], green_y[None], green_z[None],
        base_z, along, across, across_t,
    )
    spec = pl.BlockSpec(memory_space=VMEM)
    scalar = pl.BlockSpec(memory_space=pltpu.SMEM)
    still = pl.BlockSpec(memory_space=pl.ANY)
    atom, centre = pl.pallas_call(
        kernel,
        out_shape=[shape(4, ATOMS), shape(4, WC)],
        in_specs=[scalar] + [spec] * 14 + [still] * 3,
        out_specs=[spec, spec],
        scratch_shapes=SCRATCH,
        compiler_params=pltpu.CompilerParams(vmem_limit_bytes=56 << 20, collective_id=1, has_side_effects=True),
    )(*args)
    return tuple(
        pl.pallas_call(
            scale_kernel,
            out_shape=[shape(4, ATOMS), shape(4, WC)],
            in_specs=[spec] * 3,
            out_specs=[spec, spec],
        )(atom, centre, centre_charge[None])
    )


def solution(mesh):
    device = P(("gx", "gy", "gz"))
    late = P(None, ("gx", "gy", "gz"))
    tables = [jnp.asarray(t) for t in constants()]

    def run(*args):
        return jax.shard_map(
            on_device,
            mesh=mesh,
            in_specs=(P(), P(), P(), P(),
                P(("gx", "gy", "gz"), None), late, late, device,
                P(), P(), P(), P(), device, late, late, P(), P(), P(),
            ),
            out_specs=(late, late),
            check_vma=False,
        )(*tables, *args)

    return run
```
